128 devices in a mesh: band: 16 (over y_lo, z, core), grid: 8 (over x, y_hi).
Axes of the slice: x: 4, y: 4 (y_hi: 2, y_lo: 2; y = y_hi * 2 + y_lo), z: 4, core: 2. Of those that a mesh axis runs over, the one named last changes fastest.
Arguments:
- orbitals: bfloat16 [32, 192, 192, 192], P('band', 'grid'), may hold values from -6 to 6
- plan: int32 [2, 32], P(None, 'band'), may hold values from 0 to 1
Outputs:
- exchange_image: bfloat16 [32, 192, 192, 192], P('band', 'grid')
The draws below stay inside these ranges and needn't reach their ends.
Inputs may be any that keep to these rules, and one draw needn't show every extreme that they name: plan[s, i] is the position, within the partner group of band i at shift s + 1, of the band that band i pairs with.
All inputs are finite; a program needn't handle non-finite values.
Results may differ from the reference program's by a relative error of at most 0.0095.
Values may be sent and summed in bfloat16 or wider, within the bound.
No kernel may reach another device: no remote copies, remote signals or barrier semaphores. Data moves between devices by JAX's collectives and lax.ppermute only.
A program may use at most 128 MiB of HBM per device.

```python
import jax
import jax.numpy as jnp
from jax import lax

NG = 192
B_DEV = 2
SHIFTS = 2
BANDS = 32
N_BAND = 16


def with_ends(entries, key, smallest, high):
    shape = entries.shape
    spot = [jax.random.randint(jax.random.fold_in(key, axis), (), 0, shape[axis]) for axis in range(len(shape))]
    entries = entries.at[tuple(spot)].set(smallest)
    longest = shape.index(max(shape))
    spot[longest] = (spot[longest] + 1) % shape[longest]
    return entries.at[tuple(spot)].set(high)


def level_of(key, dims, split, least, top_value):
    loudness = 1.0
    for dim, shards_of in split:
        draws = jax.random.uniform(jax.random.fold_in(jax.random.fold_in(key, 6), dim), (shards_of,), jnp.float32, least / len(split), top_value / len(split))
        loudness = loudness * jnp.repeat(jnp.exp(draws), dims[dim] // shards_of).reshape((-1,) + (1,) * (len(dims) - 1 - dim))
    return loudness


def noise(rng, dims, deviation, reach, shards=(), held_as=jnp.bfloat16):
    values = jax.random.normal(rng, dims, jnp.float32) * deviation
    if len(shards) > 0:
        values = level_of(rng, dims, shards, -0.22, 0.18) * values
    return jnp.clip(values, min=-reach, max=reach).astype(held_as)


def setup_inputs(seed: int = 0) -> dict:
    key_list = jax.random.split(jax.random.key(seed), 3)
    return {
        "orbitals": noise(key_list[0], (BANDS, NG, NG, NG), 1.0, 6.0, ((0, 16), (1, 8))),
        "plan": with_ends(jax.random.randint(key_list[1], (SHIFTS, BANDS), 0, B_DEV), jax.random.fold_in(key_list[1], 1), 0, B_DEV - 1).astype(jnp.int32),
    }


screening = 0.0005


def sine_table(length):
    counts = jnp.arange(1, length + 1, dtype=jnp.float32)
    return jnp.sin(jnp.pi * counts[:, None] * counts[None, :] / (length + 1)).astype(jnp.bfloat16)


def eigen_line(modes, length):
    return 2.0 - 2.0 * jnp.cos(jnp.pi * modes / (length + 1))


def rounded(values):
    return lax.optimization_barrier(values.astype(jnp.bfloat16)).astype(jnp.float32)


def solve(density, table, kernel):
    high = lax.Precision.HIGHEST
    field = density.astype(jnp.float32)
    section = rounded(jnp.einsum("xyz,kz->xyk", field, table, precision=high))
    section = rounded(jnp.einsum("xyz,ky->xkz", section, table, precision=high))
    spectrum = jnp.einsum("xyz,kx->kyz", section, table, precision=high)
    section = rounded(spectrum * kernel)
    section = rounded(jnp.einsum("xyz,kx->kyz", section, table, precision=high))
    section = rounded(jnp.einsum("xyz,ky->xkz", section, table, precision=high))
    return jnp.einsum("xyz,kz->xyk", section, table, precision=high)


def reference(orbitals, plan):
    band_count = orbitals.shape[0]
    length = orbitals.shape[1]
    per_group = band_count // N_BAND
    table = sine_table(length).astype(jnp.float32)
    modes = jnp.arange(1, length + 1, dtype=jnp.float32)
    line = eigen_line(modes, length)
    kernel = (2.0 / (length + 1)) ** 3 / (line[:, None, None] + line[None, :, None] + line[None, None, :] + screening)
    own_sums = jnp.zeros(orbitals.shape, jnp.float32)
    for offset in range(1, SHIFTS + 1):
        def step(carry, index):
            own_acc, partner_acc = carry
            group = index // per_group
            partner = (((group + offset) % N_BAND) * per_group + plan[offset - 1, index]).astype(jnp.int32)
            first_band = orbitals[index].astype(jnp.float32)
            second_band = orbitals[partner].astype(jnp.float32)
            density = (first_band * second_band).astype(jnp.bfloat16)
            potential = solve(density, table, kernel)
            own_acc = own_acc.at[index].add(potential * second_band)
            partner_acc = partner_acc.at[partner].add(potential * first_band)
            return (own_acc, partner_acc), None

        partner_zero = jnp.zeros(orbitals.shape, jnp.float32)
        (own_sums, partner_sums), _ = lax.scan(step, (own_sums, partner_zero), jnp.arange(band_count, dtype=jnp.int32))
        own_sums = own_sums + rounded(partner_sums)
    return (-own_sums).astype(jnp.bfloat16)
```

```python
import functools

import jax
import jax.numpy as jnp
from jax import lax
from jax.experimental import pallas as pl
from jax.experimental.pallas import tpu as pltpu
from jax.sharding import PartitionSpec as P

screening = 0.0005
NG = 192
SLABS = 8
ROWS = NG // SLABS
PAIRS = 4
WIDE = PAIRS * NG
PAIRED = ROWS // 2
PIECES_IN = (6, 4, 2)
PIECES_OUT = (2, 4, 4, 2)

F32 = jnp.float32
BF16 = jnp.bfloat16
VMEM_LIMIT = 16 * 1024 * 1024

SWAP_BAND, THIRD_BAND, CORE = 0, 2, 4


def params():
    return pltpu.CompilerParams(vmem_limit_bytes=VMEM_LIMIT)


def call(kernel, grid, in_specs, out_specs, out_shape, scratch=(), aliases={}, cost=0):
    return pl.pallas_call(
        kernel,
        grid_spec=pltpu.PrefetchScalarGridSpec(
            num_scalar_prefetch=1, grid=grid, in_specs=in_specs, out_specs=out_specs, scratch_shapes=scratch
        ),
        out_shape=out_shape,
        input_output_aliases=aliases,
        compiler_params=params(),
        cost_estimate=pl.CostEstimate(flops=0, bytes_accessed=cost, transcendentals=0),
    )


def sine_table():
    counts = jnp.arange(1, NG + 1, dtype=F32)
    return jnp.sin(jnp.pi * counts[:, None] * counts[None, :] / (NG + 1)).astype(BF16)


def eigen_line(modes):
    half = jnp.sin(jnp.pi * modes / (2 * (NG + 1)))
    return 4.0 * half * half


def decay(first, second):
    mu = eigen_line(first)[:, None] + eigen_line(second)[None, :] + screening
    root = 1.0 / (1.0 + 0.5 * mu + jnp.sqrt(mu + 0.25 * mu * mu))
    return jnp.concatenate([root, root], axis=1)


def twice(block):
    return jnp.concatenate([block, block], axis=1)


def unpacked(ref, band, half):
    tail = ref[band, 0, 2].astype(F32)
    return jnp.concatenate([ref[band, 0, half].astype(F32), tail[:, 64 * half : 64 * half + 64]], axis=1)


def pack_into(ref, band, low, high):
    ref[band, 0, 0] = low[:, :128].astype(BF16)
    ref[band, 0, 1] = high[:, :128].astype(BF16)
    ref[band, 0, 2] = jnp.concatenate([low[:, 128:], high[:, 128:]], axis=1).astype(BF16)


def planes(block):
    return pl.BlockSpec((2, 2, NG, NG), lambda i, table: (0, block(i), 0, 0))


def packed(block):
    return pl.BlockSpec((2, 1, 3, NG, 128), lambda i, table: (0, block(i), 0, 0, 0))


def spectra(block):
    return pl.BlockSpec((2, NG, WIDE), lambda i, table: (block(i), 0, 0))


def whole(*shape):
    return pl.BlockSpec(shape, lambda i, table: (0,) * len(shape))


ANY = pl.BlockSpec(memory_space=pl.ANY)
STATE = jax.ShapeDtypeStruct((NG, WIDE), F32)


def pack_kernel(table, x_ref, z_ref):
    for band in range(2):
        pack_into(z_ref, band, x_ref[band, 0].astype(F32), x_ref[band, 1].astype(F32))


def pack(table, x, start, count):
    return call(
        pack_kernel,
        (count,),
        [planes(lambda i: start + i)],
        packed(lambda i: i),
        jax.ShapeDtypeStruct((2, count, 3, NG, 128), BF16),
    )(table, x)


def forward_kernel(start, first, last, table, x_ref, s_ref, z_ref, sines_ref, r_ref, log_ref, *refs):
    refs = list(refs)
    if not first:
        p_in, a_in, _ = (refs.pop(0) for _ in range(3))
    out_ref = refs.pop(0)
    results = [refs.pop(0) for _ in range(1 if last else 2)]
    p_ref, a_ref, both = refs
    step = pl.program_id(0)

    @pl.when(step == 0)
    def _():
        p_ref[...] = jnp.zeros_like(p_ref) if first else p_in[...]
        a_ref[...] = jnp.zeros_like(a_ref) if first else a_in[...]

    core = table[CORE]
    sines = sines_ref[...]
    for half in range(2):
        for band in range(2):
            both[0, band] = x_ref[band, half]
            both[1, band] = unpacked(z_ref, band, half).astype(BF16)
        rows = [both[core, q] * s_ref[table[SWAP_BAND + q], half] for q in range(2)]
        rows += [both[core, q] * both[1 - core, table[THIRD_BAND + q]] for q in range(2)]
        section = jnp.dot(jnp.concatenate(rows, axis=0), sines, preferred_element_type=F32).astype(BF16)
        section = jnp.concatenate([section[q * NG : (q + 1) * NG] for q in range(PAIRS)], axis=1)
        section = jnp.dot(sines, section, preferred_element_type=F32)
        p = twice(r_ref[...]) * p_ref[...] + section
        p_ref[...] = p
        out_ref[half] = p.astype(BF16)
        depth = (2 * (start + step) + half).astype(F32)
        a_ref[...] += twice(jnp.exp2(depth * log_ref[...])) * section

    @pl.when(step == pl.num_programs(0) - 1)
    def _():
        if last:
            results[0][:, :WIDE] = a_ref[...].astype(BF16)
            results[0][:, WIDE:] = p_ref[...].astype(BF16)
        else:
            results[0][...] = p_ref[...]
            results[1][...] = a_ref[...]


def forward(table, x, s, z, sines, r, log_r, carried, start, count):
    first, last = carried is None, start + count == PAIRED
    at = lambda i: start + i
    return call(
        functools.partial(forward_kernel, start, first, last),
        (count,),
        [planes(at), planes(at), packed(lambda i: i), whole(NG, NG), whole(NG, 2 * NG), whole(NG, 2 * NG)]
        + ([] if first else [whole(NG, WIDE), whole(NG, WIDE), ANY]),
        [spectra(at)] + ([whole(NG, 2 * WIDE)] if last else [whole(NG, WIDE)] * 2),
        [jax.ShapeDtypeStruct((ROWS, NG, WIDE), BF16)]
        + ([jax.ShapeDtypeStruct((NG, 2 * WIDE), BF16)] if last else [STATE] * 2),
        scratch=[pltpu.VMEM((NG, WIDE), F32)] * 2 + [pltpu.VMEM((2, 2, NG, NG), BF16)],
        aliases={} if first else {9: 0},
    )(table, x, s, z, sines, r, log_r, *(() if first else (carried[1], carried[2], carried[0])))


def couple_kernel(table, r_ref, in_ref, out_ref):
    r = twice(r_ref[...])
    r2 = r * r
    r4 = r2 * r2
    r8 = r4 * r4
    span = r8 * r8 * r8
    gain = r / (1.0 - r2)
    part = lambda j, k: in_ref[j * ROWS : (j + 1) * ROWS, k * WIDE : (k + 1) * WIDE].astype(F32)
    reach = [jnp.ones_like(span)]
    left = [jnp.zeros_like(span)]
    for j in range(SLABS):
        reach.append(reach[-1] * span)
        left.append(span * left[-1] + part(j, 1))
    right = [jnp.zeros_like(span)]
    for j in reversed(range(SLABS)):
        right.insert(0, span * right[0] + part(j, 0))
    full = r * reach[SLABS]
    scale = r / (1.0 - full * full)
    low = scale * (full * left[SLABS] - right[0])
    high = gain * scale * (full * right[0] - left[SLABS])
    carry = [left[j] + low * reach[j] for j in range(SLABS)]
    for j in range(SLABS):
        out_ref[j * ROWS : (j + 1) * ROWS, :WIDE] = (r * carry[j]).astype(BF16)
        if j < SLABS - 1:
            beyond = gain * (r * carry[j + 1] + right[j + 1]) + high * reach[SLABS - 1 - j]
        else:
            beyond = jnp.zeros_like(span)
        out_ref[j * ROWS : (j + 1) * ROWS, WIDE:] = beyond.astype(BF16)


def couple(table, r_local, ends):
    return call(
        couple_kernel,
        (1,),
        [whole(ROWS, 2 * NG), whole(NG, 2 * WIDE)],
        whole(NG, 2 * WIDE),
        jax.ShapeDtypeStruct((NG, 2 * WIDE), BF16),
    )(table, r_local, ends)


def spread_terms(terms, places):
    on = [place.astype(F32) for place in places]
    return [
        (1.0 - on[0]) * terms[0] + (1.0 - on[1]) * terms[1],
        on[0] * terms[0] + on[1] * terms[1],
    ]


def back_kernel(start, count, first, fresh, table, x_ref, s_ref, z_ref, sines_ref, r_ref, log_ref, p_ref, e_ref, *refs):
    refs = list(refs)
    if not first:
        u_in = refs.pop(0)
    if not fresh:
        refs = refs[2:]
    xo_ref, so_ref, zo_ref = (refs.pop(0) for _ in range(3))
    if start > 0:
        u_out = refs.pop(0)
    u_ref, both = refs
    step = pl.program_id(0)

    @pl.when(step == 0)
    def _():
        u_ref[...] = e_ref[:, WIDE:].astype(F32) if first else u_in[...]

    core = table[CORE]
    low_core = core == 0
    sines = sines_ref[...]
    kept = {}
    for half in (1, 0):
        for band in range(2):
            both[0, band] = x_ref[band, half]
            both[1, band] = unpacked(z_ref, band, half).astype(BF16)
        depth = (2 * (start + count - 1 - step) + half).astype(F32)
        carried = twice(jnp.exp2(depth * log_ref[...])) * e_ref[:, :WIDE].astype(F32)
        u = twice(r_ref[...]) * (p_ref[half].astype(F32) + u_ref[...] + carried)
        u_ref[...] = u
        section = jnp.dot(sines, u.astype(BF16), preferred_element_type=F32).astype(BF16)
        section = jnp.concatenate([section[:, q * NG : (q + 1) * NG] for q in range(PAIRS)], axis=0)
        potential = jnp.dot(section, sines, preferred_element_type=F32)
        v = [potential[q * NG : (q + 1) * NG] for q in range(PAIRS)]
        f = [both[core, q].astype(F32) for q in range(2)]
        s = [s_ref[table[SWAP_BAND + q], half].astype(F32) for q in range(2)]
        t = [both[1 - core, table[THIRD_BAND + q]].astype(F32) for q in range(2)]
        own = [v[q] * s[q] + v[2 + q] * t[q] for q in range(2)]
        swap = spread_terms([v[q] * f[q] for q in range(2)], [table[SWAP_BAND + q] for q in range(2)])
        third = spread_terms([v[2 + q] * f[q] for q in range(2)], [table[THIRD_BAND + q] for q in range(2)])
        for j in range(2):
            xo_ref[j, half] = jnp.where(low_core, own[j], third[j]).astype(BF16)
            so_ref[j, half] = swap[j].astype(BF16)
            kept[j, half] = jnp.where(low_core, third[j], own[j])
    for j in range(2):
        pack_into(zo_ref, j, kept[j, 0], kept[j, 1])

    if start > 0:

        @pl.when(step == count - 1)
        def _():
            u_out[...] = u_ref[...]


def back(table, x, s, z, z_start, sines, r, log_r, p, edges, u, sums, base, size, start, count):
    first, fresh = u is None, sums is None
    at = lambda i: start + count - 1 - i
    in_sums = lambda i: at(i) - base
    outs = call(
        functools.partial(back_kernel, start, count, first, fresh),
        (count,),
        [
            planes(at),
            planes(at),
            packed(lambda i: at(i) - z_start),
            whole(NG, NG),
            whole(NG, 2 * NG),
            whole(NG, 2 * NG),
            spectra(at),
            whole(NG, 2 * WIDE),
        ]
        + ([] if first else [whole(NG, WIDE)])
        + ([] if fresh else [ANY, ANY]),
        [planes(in_sums), planes(in_sums), packed(lambda i: count - 1 - i)] + ([whole(NG, WIDE)] if start > 0 else []),
        [jax.ShapeDtypeStruct((2, 2 * size, NG, NG), BF16)] * 2
        + [jax.ShapeDtypeStruct((2, count, 3, NG, 128), BF16)]
        + ([STATE] if start > 0 else []),
        scratch=[pltpu.VMEM((NG, WIDE), F32), pltpu.VMEM((2, 2, NG, NG), BF16)],
        aliases={} if fresh else {10 - first: 0, 11 - first: 1},
        cost=0,
    )(table, x, s, z, sines, r, log_r, p, edges, *(() if first else (u,)), *(() if fresh else sums))
    return outs[:2], outs[2], outs[3] if start > 0 else None


def close_kernel(scale, table, x_ref, s_ref, z_ref, *refs):
    for half in range(2):
        for band in range(2):
            total = x_ref[band, half].astype(F32) + s_ref[band, half].astype(F32) + unpacked(z_ref, band, half)
            refs[-1][band, half] = (scale * total).astype(BF16)


def close(scale, table, xo, so, zo, out, base, start, count):
    from_sums = planes(lambda i: start - base + i)
    more = [] if out is None else [out]
    return call(
        functools.partial(close_kernel, scale),
        (count,),
        [from_sums, from_sums, packed(lambda i: i)] + [ANY] * len(more),
        planes(lambda i: start + i),
        jax.ShapeDtypeStruct((2, ROWS, NG, NG), BF16),
        aliases={4: 0} if more else {},
    )(table, xo, so, zo, *more)


def placed(pieces):
    return [(sum(pieces[:k]), pieces[k]) for k in range(len(pieces))]


def shards(orbitals, plan):
    groups = lax.axis_size("band")
    core = lax.axis_index("band") % 2
    place = lax.axis_index("grid")
    moved = lambda step: [(g, step(g) % groups) for g in range(groups)]
    out_way = moved(lambda g: g - 2 if g % 2 == 0 else g + 2)
    home_way = moved(lambda g: g + 2 if g % 2 == 0 else g - 2)
    across = moved(lambda g: g + 1 if g % 2 == 0 else g - 1)
    exchange = lambda block: lax.all_to_all(block, "grid", split_axis=0, concat_axis=0, tiled=True)

    plan_left = lax.ppermute(plan, "band", moved(lambda g: g + 2))
    swapped = lax.ppermute(orbitals, "band", across)
    table = jnp.concatenate(
        [jnp.where(core == 0, plan, plan_left).reshape(-1), core[None].astype(jnp.int32)]
    )
    arrived = [
        (start, count, lax.ppermute(pack(plan[0], orbitals, start, count), "band", out_way))
        for start, count in placed(PIECES_IN)
    ]

    sines = sine_table()
    modes = jnp.arange(1, NG + 1, dtype=F32)
    root = decay(modes, modes)
    log_root = jnp.log2(root)
    local_modes = (place * ROWS + jnp.arange(1, ROWS + 1, dtype=jnp.int32)).astype(F32)
    root_local = decay(local_modes, modes)

    carried = None
    for start, count, z in arrived:
        carried = forward(table, orbitals, swapped, z, sines, root, log_root, carried, start, count)
    held, ends = carried
    edges = exchange(couple(table, root_local, exchange(ends)))

    scale = -((2.0 / (NG + 1)) ** 2)
    u, parts = None, []
    for start, count in reversed(placed(PIECES_OUT)):
        if len(parts) == 2:
            (so, zo), u = lax.optimization_barrier((parts[0][1:3], u))
            parts[0] = (parts[0][0], so, zo, *parts[0][3:])
        z_start, z = [(at, z) for at, many, z in arrived if at <= start and start + count <= at + many][0]
        (xo, so), zo, u = back(
            table, orbitals, swapped, z, z_start, sines, root, log_root, held, edges, u, None, start, count, start, count
        )
        parts.append((xo, lax.ppermute(so, "band", across), lax.ppermute(zo, "band", home_way), start, count))
    out = None
    for xo, so, zo, start, count in parts:
        out = close(scale, table, xo, so, zo, out, start, start, count)
    return out


def solution(mesh):
    return jax.shard_map(
        shards,
        mesh=mesh,
        in_specs=(P("band", "grid", None, None), P(None, "band")),
        out_specs=P("band", "grid", None, None),
        check_vma=False,
    )
```

```python
import functools

import jax
import jax.numpy as jnp
from jax import lax
from jax.experimental import pallas as pl
from jax.experimental.pallas import tpu as pltpu
from jax.sharding import PartitionSpec as P

screening = 0.0005
NG = 192
SLABS = 8
ROWS = NG // SLABS
PAIRS = 4
WIDE = PAIRS * NG
PAIRED = ROWS // 2
PIECES_IN = (6, 4, 2)
PIECES_OUT = (1, 3, 5, 3)
PACKED = 2

F32 = jnp.float32
BF16 = jnp.bfloat16
VMEM_LIMIT = 16 * 1024 * 1024

SWAP_BAND, THIRD_BAND, CORE = 0, 2, 4


def params():
    return pltpu.CompilerParams(vmem_limit_bytes=VMEM_LIMIT)


def call(kernel, grid, in_specs, out_specs, out_shape, scratch=(), aliases={}, cost=0):
    return pl.pallas_call(
        kernel,
        grid_spec=pltpu.PrefetchScalarGridSpec(
            num_scalar_prefetch=1, grid=grid, in_specs=in_specs, out_specs=out_specs, scratch_shapes=scratch
        ),
        out_shape=out_shape,
        input_output_aliases=aliases,
        compiler_params=params(),
        cost_estimate=pl.CostEstimate(flops=0, bytes_accessed=cost, transcendentals=0),
    )


def sine_table():
    counts = jnp.arange(1, NG + 1, dtype=F32)
    return jnp.sin(jnp.pi * counts[:, None] * counts[None, :] / (NG + 1)).astype(BF16)


def eigen_line(modes):
    half = jnp.sin(jnp.pi * modes / (2 * (NG + 1)))
    return 4.0 * half * half


def decay(first, second):
    mu = eigen_line(first)[:, None] + eigen_line(second)[None, :] + screening
    root = 1.0 / (1.0 + 0.5 * mu + jnp.sqrt(mu + 0.25 * mu * mu))
    return jnp.concatenate([root, root], axis=1)


def twice(block):
    return jnp.concatenate([block, block], axis=1)


def unpacked(ref, band, half):
    tail = ref[band, 0, 2].astype(F32)
    return jnp.concatenate([ref[band, 0, half].astype(F32), tail[:, 64 * half : 64 * half + 64]], axis=1)


def pack_into(ref, band, low, high):
    ref[band, 0, 0] = low[:, :128].astype(BF16)
    ref[band, 0, 1] = high[:, :128].astype(BF16)
    ref[band, 0, 2] = jnp.concatenate([low[:, 128:], high[:, 128:]], axis=1).astype(BF16)


def planes(block):
    return pl.BlockSpec((2, 2, NG, NG), lambda i, table: (0, block(i), 0, 0))


def packed(block):
    return pl.BlockSpec((2, 1, 3, NG, 128), lambda i, table: (0, block(i), 0, 0, 0))


def spectra(block):
    return pl.BlockSpec((2, NG, WIDE), lambda i, table: (block(i), 0, 0))


def whole(*shape):
    return pl.BlockSpec(shape, lambda i, table: (0,) * len(shape))


ANY = pl.BlockSpec(memory_space=pl.ANY)
STATE = jax.ShapeDtypeStruct((NG, WIDE), F32)


def in_hbm(block):
    return pltpu.with_memory_space_constraint(block, pltpu.HBM)


def pack_kernel(table, x_ref, z_ref):
    for band in range(2):
        for pair in range(PACKED):
            low, high = 2 * pair, 2 * pair + 1
            z_ref[band, pair, 0] = x_ref[band, low, :, :128]
            z_ref[band, pair, 1] = x_ref[band, high, :, :128]
            tails = [x_ref[band, plane, :, 128:].astype(F32) for plane in (low, high)]
            z_ref[band, pair, 2] = jnp.concatenate(tails, axis=1).astype(BF16)


def pack(table, x, start, count):
    return call(
        pack_kernel,
        (count // PACKED,),
        [pl.BlockSpec((2, 2 * PACKED, NG, NG), lambda i, table: (0, start // PACKED + i, 0, 0))],
        pl.BlockSpec((2, PACKED, 3, NG, 128), lambda i, table: (0, i, 0, 0, 0)),
        jax.ShapeDtypeStruct((2, count, 3, NG, 128), BF16),
    )(table, in_hbm(x))


def forward_kernel(start, first, last, table, x_ref, s_ref, z_ref, sines_ref, r_ref, log_ref, *refs):
    refs = list(refs)
    if not first:
        p_in, a_in, _ = (refs.pop(0) for _ in range(3))
    out_ref = refs.pop(0)
    results = [refs.pop(0) for _ in range(1 if last else 2)]
    p_ref, a_ref, both = refs
    step = pl.program_id(0)

    @pl.when(step == 0)
    def _():
        p_ref[...] = jnp.zeros_like(p_ref) if first else p_in[...]
        a_ref[...] = jnp.zeros_like(a_ref) if first else a_in[...]

    core = table[CORE]
    sines = sines_ref[...]
    for half in range(2):
        for band in range(2):
            both[0, band] = x_ref[band, half]
            both[1, band] = unpacked(z_ref, band, half).astype(BF16)
        rows = [both[core, q] * s_ref[table[SWAP_BAND + q], half] for q in range(2)]
        rows += [both[core, q] * both[1 - core, table[THIRD_BAND + q]] for q in range(2)]
        section = jnp.dot(jnp.concatenate(rows, axis=0), sines, preferred_element_type=F32).astype(BF16)
        section = jnp.concatenate([section[q * NG : (q + 1) * NG] for q in range(PAIRS)], axis=1)
        section = jnp.dot(sines, section, preferred_element_type=F32)
        p = twice(r_ref[...]) * p_ref[...] + section
        p_ref[...] = p
        out_ref[half] = p.astype(BF16)
        depth = (2 * (start + step) + half).astype(F32)
        a_ref[...] += twice(jnp.exp2(depth * log_ref[...])) * section

    @pl.when(step == pl.num_programs(0) - 1)
    def _():
        if last:
            results[0][:, :WIDE] = a_ref[...].astype(BF16)
            results[0][:, WIDE:] = p_ref[...].astype(BF16)
        else:
            results[0][...] = p_ref[...]
            results[1][...] = a_ref[...]


def forward(table, x, s, z, sines, r, log_r, carried, start, count):
    first, last = carried is None, start + count == PAIRED
    at = lambda i: start + i
    return call(
        functools.partial(forward_kernel, start, first, last),
        (count,),
        [planes(at), planes(at), packed(lambda i: i), whole(NG, NG), whole(NG, 2 * NG), whole(NG, 2 * NG)]
        + ([] if first else [whole(NG, WIDE), whole(NG, WIDE), ANY]),
        [spectra(at)] + ([whole(NG, 2 * WIDE)] if last else [whole(NG, WIDE)] * 2),
        [pltpu.HBM((ROWS, NG, WIDE), BF16)] + ([jax.ShapeDtypeStruct((NG, 2 * WIDE), BF16)] if last else [STATE] * 2),
        scratch=[pltpu.VMEM((NG, WIDE), F32)] * 2 + [pltpu.VMEM((2, 2, NG, NG), BF16)],
        aliases={} if first else {9: 0},
    )(table, x, s, z, sines, r, log_r, *(() if first else (carried[1], carried[2], carried[0])))


def couple_kernel(table, r_ref, in_ref, out_ref):
    r = twice(r_ref[...])
    r2 = r * r
    r4 = r2 * r2
    r8 = r4 * r4
    span = r8 * r8 * r8
    gain = r / (1.0 - r2)
    part = lambda j, k: in_ref[j * ROWS : (j + 1) * ROWS, k * WIDE : (k + 1) * WIDE].astype(F32)
    reach = [jnp.ones_like(span)]
    left = [jnp.zeros_like(span)]
    for j in range(SLABS):
        reach.append(reach[-1] * span)
        left.append(span * left[-1] + part(j, 1))
    right = [jnp.zeros_like(span)]
    for j in reversed(range(SLABS)):
        right.insert(0, span * right[0] + part(j, 0))
    full = r * reach[SLABS]
    scale = r / (1.0 - full * full)
    low = scale * (full * left[SLABS] - right[0])
    high = gain * scale * (full * right[0] - left[SLABS])
    carry = [left[j] + low * reach[j] for j in range(SLABS)]
    for j in range(SLABS):
        out_ref[j * ROWS : (j + 1) * ROWS, :WIDE] = (r * carry[j]).astype(BF16)
        if j < SLABS - 1:
            beyond = gain * (r * carry[j + 1] + right[j + 1]) + high * reach[SLABS - 1 - j]
        else:
            beyond = jnp.zeros_like(span)
        out_ref[j * ROWS : (j + 1) * ROWS, WIDE:] = beyond.astype(BF16)


def couple(table, r_local, ends):
    return call(
        couple_kernel,
        (1,),
        [whole(ROWS, 2 * NG), whole(NG, 2 * WIDE)],
        whole(NG, 2 * WIDE),
        jax.ShapeDtypeStruct((NG, 2 * WIDE), BF16),
    )(table, r_local, ends)


def spread_terms(terms, places):
    apart = jnp.where(places[0] == places[1], 0.0, 1.0)
    other = apart * terms[1]
    return [terms[0] + (terms[1] - other), other]


def back_kernel(start, count, first, fresh, table, x_ref, s_ref, z_ref, sines_ref, r_ref, log_ref, p_ref, e_ref, *refs):
    refs = list(refs)
    if not first:
        u_in = refs.pop(0)
    if not fresh:
        refs = refs[2:]
    xo_ref, so_ref, zo_ref = (refs.pop(0) for _ in range(3))
    if start > 0:
        u_out = refs.pop(0)
    u_ref, both = refs
    step = pl.program_id(0)

    @pl.when(step == 0)
    def _():
        u_ref[...] = e_ref[:, WIDE:].astype(F32) if first else u_in[...]

    core = table[CORE]
    low_core = core == 0
    sines = sines_ref[...]
    kept = {}
    for half in (1, 0):
        for band in range(2):
            both[0, band] = x_ref[band, half]
            both[1, band] = unpacked(z_ref, band, half).astype(BF16)
        depth = (2 * (start + count - 1 - step) + half).astype(F32)
        carried = twice(jnp.exp2(depth * log_ref[...])) * e_ref[:, :WIDE].astype(F32)
        u = twice(r_ref[...]) * (p_ref[half].astype(F32) + u_ref[...] + carried)
        u_ref[...] = u
        section = jnp.dot(sines, u.astype(BF16), preferred_element_type=F32).astype(BF16)
        section = jnp.concatenate([section[:, q * NG : (q + 1) * NG] for q in range(PAIRS)], axis=0)
        potential = jnp.dot(section, sines, preferred_element_type=F32)
        v = [potential[q * NG : (q + 1) * NG] for q in range(PAIRS)]
        f = [both[core, q].astype(F32) for q in range(2)]
        s = [s_ref[table[SWAP_BAND + q], half].astype(F32) for q in range(2)]
        t = [both[1 - core, table[THIRD_BAND + q]].astype(F32) for q in range(2)]
        own = [v[q] * s[q] + v[2 + q] * t[q] for q in range(2)]
        swap = spread_terms([v[q] * f[q] for q in range(2)], [table[SWAP_BAND + q] for q in range(2)])
        third = spread_terms([v[2 + q] * f[q] for q in range(2)], [table[THIRD_BAND + q] for q in range(2)])
        swap_at, third_at = table[SWAP_BAND], table[THIRD_BAND]
        own_at, sent_at = jnp.where(low_core, 0, third_at), jnp.where(low_core, third_at, 0)
        for j in range(2):
            xo_ref[jnp.abs(own_at - j), half] = jnp.where(low_core, own[j], third[j]).astype(BF16)
            so_ref[jnp.abs(swap_at - j), half] = swap[j].astype(BF16)
            kept[j, half] = jnp.where(low_core, third[j], own[j])
    for j in range(2):
        pack_into(zo_ref, jnp.abs(sent_at - j), kept[j, 0], kept[j, 1])

    if start > 0:

        @pl.when(step == count - 1)
        def _():
            u_out[...] = u_ref[...]


def back(table, x, s, z, z_start, sines, r, log_r, p, edges, u, sums, base, size, start, count):
    first, fresh = u is None, sums is None
    at = lambda i: start + count - 1 - i
    in_sums = lambda i: at(i) - base
    outs = call(
        functools.partial(back_kernel, start, count, first, fresh),
        (count,),
        [
            planes(at),
            planes(at),
            packed(lambda i: at(i) - z_start),
            whole(NG, NG),
            whole(NG, 2 * NG),
            whole(NG, 2 * NG),
            spectra(at),
            whole(NG, 2 * WIDE),
        ]
        + ([] if first else [whole(NG, WIDE)])
        + ([] if fresh else [ANY, ANY]),
        [planes(in_sums), planes(in_sums), packed(lambda i: count - 1 - i)] + ([whole(NG, WIDE)] if start > 0 else []),
        [jax.ShapeDtypeStruct((2, 2 * size, NG, NG), BF16)] * 2
        + [jax.ShapeDtypeStruct((2, count, 3, NG, 128), BF16)]
        + ([STATE] if start > 0 else []),
        scratch=[pltpu.VMEM((NG, WIDE), F32), pltpu.VMEM((2, 2, NG, NG), BF16)],
        aliases={} if fresh else {10 - first: 0, 11 - first: 1},
        cost=0,
    )(table, *(in_hbm(block) for block in (x, s, z, sines, r, log_r, p, edges)), *(() if first else (u,)), *(() if fresh else sums))
    return outs[:2], outs[2], outs[3] if start > 0 else None


def close_kernel(scale, table, x_ref, s_ref, z_ref, *refs):
    for half in range(2):
        for band in range(2):
            total = x_ref[band, half].astype(F32) + s_ref[band, half].astype(F32) + unpacked(z_ref, band, half)
            refs[-1][band, half] = (scale * total).astype(BF16)


def close(scale, table, xo, so, zo, out, base, start, count):
    from_sums = planes(lambda i: start - base + i)
    more = [] if out is None else [out]
    return call(
        functools.partial(close_kernel, scale),
        (count,),
        [from_sums, from_sums, packed(lambda i: i)] + [ANY] * len(more),
        planes(lambda i: start + i),
        jax.ShapeDtypeStruct((2, ROWS, NG, NG), BF16),
        aliases={4: 0} if more else {},
    )(table, xo, so, zo, *more)


def placed(pieces):
    return [(sum(pieces[:k]), pieces[k]) for k in range(len(pieces))]


def shards(orbitals, plan):
    groups = lax.axis_size("band")
    core = lax.axis_index("band") % 2
    place = lax.axis_index("grid")
    moved = lambda step: [(g, step(g) % groups) for g in range(groups)]
    out_way = moved(lambda g: g - 2 if g % 2 == 0 else g + 2)
    home_way = moved(lambda g: g + 2 if g % 2 == 0 else g - 2)
    across = moved(lambda g: g + 1 if g % 2 == 0 else g - 1)
    exchange = lambda block: lax.all_to_all(block, "grid", split_axis=0, concat_axis=0, tiled=True)

    swapped = lax.ppermute(orbitals, "band", across)
    plan_left = lax.ppermute(lax.ppermute(plan, "band", across), "band", moved(lambda g: g + 3 if g % 2 == 0 else g - 3))
    table = jnp.concatenate(
        [jnp.where(core == 0, plan, plan_left).reshape(-1), core[None].astype(jnp.int32)]
    )
    arrived = []
    for start, count in placed(PIECES_IN):
        piece = pack(plan[0], orbitals, start, count)
        arrived.append((start, count, lax.ppermute(piece, "band", out_way)))

    sines = sine_table()
    modes = jnp.arange(1, NG + 1, dtype=F32)
    root = decay(modes, modes)
    log_root = jnp.log2(root)
    local_modes = (place * ROWS + jnp.arange(1, ROWS + 1, dtype=jnp.int32)).astype(F32)
    root_local = decay(local_modes, modes)

    carried = None
    for start, count, z in arrived:
        carried = forward(table, orbitals, swapped, z, sines, root, log_root, carried, start, count)
    held, ends = carried
    edges = exchange(couple(table, root_local, exchange(ends)))

    scale = -((2.0 / (NG + 1)) ** 2)
    joined = jnp.concatenate([z for _, _, z in arrived], axis=1)
    u, parts = None, []
    for start, count in reversed(placed(PIECES_OUT)):
        if len(parts) == 2:
            xo, so, zo, *where = parts[-2]
            so, zo, u = lax.optimization_barrier((so, zo, u))
            parts[-2] = (xo, so, zo, *where)
        (xo, so), zo, u = back(
            table, orbitals, swapped, joined, 0, sines, root, log_root, held, edges, u, None, start, count, start, count
        )
        parts.append((xo, lax.ppermute(so, "band", across), lax.ppermute(zo, "band", home_way), start, count))
    out = None
    for xo, so, zo, start, count in parts:
        out = close(scale, table, xo, so, zo, out, start, start, count)
    return out


def solution(mesh):
    return jax.shard_map(
        shards,
        mesh=mesh,
        in_specs=(P("band", "grid", None, None), P(None, "band")),
        out_specs=P("band", "grid", None, None),
        check_vma=False,
    )
```

```python
import functools

import jax
import jax.numpy as jnp
from jax import lax
from jax.experimental import pallas as pl
from jax.experimental.pallas import tpu as pltpu
from jax.sharding import PartitionSpec as P

screening = 0.0005
NG = 192
SLABS = 8
ROWS = NG // SLABS
PAIRS = 4
WIDE = PAIRS * NG
PAIRED = ROWS // 2
PIECES_IN = (6, 4, 2)
PIECES_OUT = (1, 3, 5, 3)
WAITS = (2,)

F32 = jnp.float32
BF16 = jnp.bfloat16
VMEM_LIMIT = 16 * 1024 * 1024

SWAP_BAND, THIRD_BAND, CORE = 0, 2, 4


def params():
    return pltpu.CompilerParams(vmem_limit_bytes=VMEM_LIMIT)


def call(kernel, grid, in_specs, out_specs, out_shape, scratch=(), aliases={}, cost=0):
    return pl.pallas_call(
        kernel,
        grid_spec=pltpu.PrefetchScalarGridSpec(
            num_scalar_prefetch=1, grid=grid, in_specs=in_specs, out_specs=out_specs, scratch_shapes=scratch
        ),
        out_shape=out_shape,
        input_output_aliases=aliases,
        compiler_params=params(),
        cost_estimate=pl.CostEstimate(flops=0, bytes_accessed=cost, transcendentals=0),
    )


def sine_table():
    counts = jnp.arange(1, NG + 1, dtype=F32)
    return jnp.sin(jnp.pi * counts[:, None] * counts[None, :] / (NG + 1)).astype(BF16)


def eigen_line(modes):
    half = jnp.sin(jnp.pi * modes / (2 * (NG + 1)))
    return 4.0 * half * half


def decay(first, second):
    mu = eigen_line(first)[:, None] + eigen_line(second)[None, :] + screening
    root = 1.0 / (1.0 + 0.5 * mu + jnp.sqrt(mu + 0.25 * mu * mu))
    return jnp.concatenate([root, root], axis=1)


def twice(block):
    return jnp.concatenate([block, block], axis=1)


def unpacked(ref, band, half):
    tail = ref[band, 0, 2].astype(F32)
    return jnp.concatenate([ref[band, 0, half].astype(F32), tail[:, 64 * half : 64 * half + 64]], axis=1)


def pack_into(ref, band, low, high):
    ref[band, 0, 0] = low[:, :128].astype(BF16)
    ref[band, 0, 1] = high[:, :128].astype(BF16)
    ref[band, 0, 2] = jnp.concatenate([low[:, 128:], high[:, 128:]], axis=1).astype(BF16)


def planes(block):
    return pl.BlockSpec((2, 2, NG, NG), lambda i, table: (0, block(i), 0, 0))


def packed(block):
    return pl.BlockSpec((2, 1, 3, NG, 128), lambda i, table: (0, block(i), 0, 0, 0))


def spectra(block):
    return pl.BlockSpec((2, NG, WIDE), lambda i, table: (block(i), 0, 0))


def whole(*shape):
    return pl.BlockSpec(shape, lambda i, table: (0,) * len(shape))


ANY = pl.BlockSpec(memory_space=pl.ANY)
STATE = jax.ShapeDtypeStruct((NG, WIDE), F32)


def in_hbm(block):
    return pltpu.with_memory_space_constraint(block, pltpu.HBM)


def pack_kernel(start, count, x_ref, z_ref, planes_in, packed_out, sems_in, sems_out):
    def fetch(i):
        return pltpu.make_async_copy(x_ref.at[:, pl.ds(2 * (start + i), 2)], planes_in.at[i], sems_in.at[i])

    def store(i):
        return pltpu.make_async_copy(packed_out.at[i], z_ref.at[:, i], sems_out.at[i])

    for i in range(count):
        fetch(i).start()
    for i in range(count):
        fetch(i).wait()
        for band in range(2):
            for half in range(2):
                packed_out[i, band, half] = planes_in[i, band, half, :, :128]
            tails = [planes_in[i, band, half, :, 128:].astype(F32) for half in range(2)]
            packed_out[i, band, 2] = jnp.concatenate(tails, axis=1).astype(BF16)
        store(i).start()
    for i in range(count):
        store(i).wait()


def pack(x, start, count):
    return pl.pallas_call(
        functools.partial(pack_kernel, start, count),
        in_specs=[ANY],
        out_specs=ANY,
        out_shape=jax.ShapeDtypeStruct((2, count, 3, NG, 128), BF16),
        scratch_shapes=[
            pltpu.VMEM((count, 2, 2, NG, NG), BF16),
            pltpu.VMEM((count, 2, 3, NG, 128), BF16),
            pltpu.SemaphoreType.DMA((count,)),
            pltpu.SemaphoreType.DMA((count,)),
        ],
        compiler_params=params(),
        cost_estimate=pl.CostEstimate(flops=0, bytes_accessed=0, transcendentals=0),
    )(in_hbm(x))


def forward_kernel(start, first, last, table, x_ref, s_ref, z_ref, sines_ref, r_ref, log_ref, *refs):
    refs = list(refs)
    if not first:
        p_in, a_in, _ = (refs.pop(0) for _ in range(3))
    out_ref = refs.pop(0)
    results = [refs.pop(0) for _ in range(1 if last else 2)]
    p_ref, a_ref, both = refs
    step = pl.program_id(0)

    @pl.when(step == 0)
    def _():
        p_ref[...] = jnp.zeros_like(p_ref) if first else p_in[...]
        a_ref[...] = jnp.zeros_like(a_ref) if first else a_in[...]

    core = table[CORE]
    sines = sines_ref[...]
    for half in range(2):
        for band in range(2):
            both[0, band] = x_ref[band, half]
            both[1, band] = unpacked(z_ref, band, half).astype(BF16)
        rows = [both[core, q] * s_ref[table[SWAP_BAND + q], half] for q in range(2)]
        rows += [both[core, q] * both[1 - core, table[THIRD_BAND + q]] for q in range(2)]
        section = jnp.dot(jnp.concatenate(rows, axis=0), sines, preferred_element_type=F32).astype(BF16)
        section = jnp.concatenate([section[q * NG : (q + 1) * NG] for q in range(PAIRS)], axis=1)
        section = jnp.dot(sines, section, preferred_element_type=F32)
        p = twice(r_ref[...]) * p_ref[...] + section
        p_ref[...] = p
        out_ref[half] = p.astype(BF16)
        depth = (2 * (start + step) + half).astype(F32)
        a_ref[...] += twice(jnp.exp2(depth * log_ref[...])) * section

    @pl.when(step == pl.num_programs(0) - 1)
    def _():
        if last:
            results[0][:, :WIDE] = a_ref[...].astype(BF16)
            results[0][:, WIDE:] = p_ref[...].astype(BF16)
        else:
            results[0][...] = p_ref[...]
            results[1][...] = a_ref[...]


def forward(table, x, s, z, sines, r, log_r, carried, start, count):
    first, last = carried is None, start + count == PAIRED
    at = lambda i: start + i
    return call(
        functools.partial(forward_kernel, start, first, last),
        (count,),
        [planes(at), planes(at), packed(lambda i: i), whole(NG, NG), whole(NG, 2 * NG), whole(NG, 2 * NG)]
        + ([] if first else [whole(NG, WIDE), whole(NG, WIDE), ANY]),
        [spectra(at)] + ([whole(NG, 2 * WIDE)] if last else [whole(NG, WIDE)] * 2),
        [pltpu.HBM((ROWS, NG, WIDE), BF16)] + ([pltpu.HBM((NG, 2 * WIDE), BF16)] if last else [STATE] * 2),
        scratch=[pltpu.VMEM((NG, WIDE), F32)] * 2 + [pltpu.VMEM((2, 2, NG, NG), BF16)],
        aliases={} if first else {9: 0},
    )(table, x, s, z, sines, r, log_r, *(() if first else (carried[1], carried[2], carried[0])))


def couple_kernel(table, r_ref, in_ref, out_ref):
    r = twice(r_ref[...])
    r2 = r * r
    r4 = r2 * r2
    r8 = r4 * r4
    span = r8 * r8 * r8
    gain = r / (1.0 - r2)
    part = lambda j, k: in_ref[j * ROWS : (j + 1) * ROWS, k * WIDE : (k + 1) * WIDE].astype(F32)
    reach = [jnp.ones_like(span)]
    left = [jnp.zeros_like(span)]
    for j in range(SLABS):
        reach.append(reach[-1] * span)
        left.append(span * left[-1] + part(j, 1))
    right = [jnp.zeros_like(span)]
    for j in reversed(range(SLABS)):
        right.insert(0, span * right[0] + part(j, 0))
    full = r * reach[SLABS]
    scale = r / (1.0 - full * full)
    low = scale * (full * left[SLABS] - right[0])
    high = gain * scale * (full * right[0] - left[SLABS])
    carry = [left[j] + low * reach[j] for j in range(SLABS)]
    for j in range(SLABS):
        out_ref[j * ROWS : (j + 1) * ROWS, :WIDE] = (r * carry[j]).astype(BF16)
        if j < SLABS - 1:
            beyond = gain * (r * carry[j + 1] + right[j + 1]) + high * reach[SLABS - 1 - j]
        else:
            beyond = jnp.zeros_like(span)
        out_ref[j * ROWS : (j + 1) * ROWS, WIDE:] = beyond.astype(BF16)


def couple(table, r_local, ends):
    return call(
        couple_kernel,
        (1,),
        [whole(ROWS, 2 * NG), whole(NG, 2 * WIDE)],
        whole(NG, 2 * WIDE),
        jax.ShapeDtypeStruct((NG, 2 * WIDE), BF16),
    )(table, r_local, ends)


def spread_terms(terms, places):
    apart = jnp.where(places[0] == places[1], 0.0, 1.0)
    other = apart * terms[1]
    return [terms[0] + (terms[1] - other), other]


def back_kernel(start, count, first, table, x_ref, s_ref, z_ref, sines_ref, r_ref, log_ref, p_ref, e_ref, *refs):
    refs = list(refs)
    if not first:
        u_in = refs.pop(0)
    xo_ref, so_ref, zo_ref = (refs.pop(0) for _ in range(3))
    if start > 0:
        u_out = refs.pop(0)
    u_ref, both = refs
    step = pl.program_id(0)

    @pl.when(step == 0)
    def _():
        u_ref[...] = e_ref[:, WIDE:].astype(F32) if first else u_in[...]

    core = table[CORE]
    low_core = core == 0
    sines = sines_ref[...]
    kept, given = {}, {}
    for half in (1, 0):
        for band in range(2):
            both[0, band] = x_ref[band, half]
            both[1, band] = unpacked(z_ref, band, half).astype(BF16)
        depth = (2 * (start + count - 1 - step) + half).astype(F32)
        carried = twice(jnp.exp2(depth * log_ref[...])) * e_ref[:, :WIDE].astype(F32)
        u = twice(r_ref[...]) * (p_ref[half].astype(F32) + u_ref[...] + carried)
        u_ref[...] = u
        section = jnp.dot(sines, u.astype(BF16), preferred_element_type=F32).astype(BF16)
        section = jnp.concatenate([section[:, q * NG : (q + 1) * NG] for q in range(PAIRS)], axis=0)
        potential = jnp.dot(section, sines, preferred_element_type=F32)
        v = [potential[q * NG : (q + 1) * NG] for q in range(PAIRS)]
        f = [both[core, q].astype(F32) for q in range(2)]
        s = [s_ref[table[SWAP_BAND + q], half].astype(F32) for q in range(2)]
        t = [both[1 - core, table[THIRD_BAND + q]].astype(F32) for q in range(2)]
        own = [v[q] * s[q] + v[2 + q] * t[q] for q in range(2)]
        swap = spread_terms([v[q] * f[q] for q in range(2)], [table[SWAP_BAND + q] for q in range(2)])
        third = spread_terms([v[2 + q] * f[q] for q in range(2)], [table[THIRD_BAND + q] for q in range(2)])
        swap_at, third_at = table[SWAP_BAND], table[THIRD_BAND]
        own_at, sent_at = jnp.where(low_core, 0, third_at), jnp.where(low_core, third_at, 0)
        for j in range(2):
            xo_ref[jnp.abs(own_at - j), half] = jnp.where(low_core, own[j], third[j]).astype(BF16)
            given[j, half] = swap[j]
            kept[j, half] = jnp.where(low_core, third[j], own[j])
    for j in range(2):
        pack_into(so_ref, jnp.abs(swap_at - j), given[j, 0], given[j, 1])
        pack_into(zo_ref, jnp.abs(sent_at - j), kept[j, 0], kept[j, 1])

    if start > 0:

        @pl.when(step == count - 1)
        def _():
            u_out[...] = u_ref[...]


def back(table, x, s, z, sines, r, log_r, p, edges, u, start, count):
    first = u is None
    at = lambda i: start + count - 1 - i
    local = lambda i: count - 1 - i
    outs = call(
        functools.partial(back_kernel, start, count, first),
        (count,),
        [
            planes(at),
            planes(at),
            packed(at),
            whole(NG, NG),
            whole(NG, 2 * NG),
            whole(NG, 2 * NG),
            spectra(at),
            whole(NG, 2 * WIDE),
        ]
        + ([] if first else [whole(NG, WIDE)]),
        [planes(local), packed(local), packed(local)] + ([whole(NG, WIDE)] if start > 0 else []),
        [jax.ShapeDtypeStruct((2, 2 * count, NG, NG), BF16)]
        + [jax.ShapeDtypeStruct((2, count, 3, NG, 128), BF16)] * 2
        + ([STATE] if start > 0 else []),
        scratch=[pltpu.VMEM((NG, WIDE), F32), pltpu.VMEM((2, 2, NG, NG), BF16)],
    )(table, *(in_hbm(block) for block in (x, s, z, sines, r, log_r, p, edges)), *(() if first else (u,)))
    return outs[:3], outs[3] if start > 0 else None


def close_kernel(scale, table, x_ref, s_ref, z_ref, *refs):
    for half in range(2):
        for band in range(2):
            total = x_ref[band, half].astype(F32) + unpacked(s_ref, band, half) + unpacked(z_ref, band, half)
            refs[-1][band, half] = (scale * total).astype(BF16)


def close(scale, table, xo, so, zo, out, start, count):
    same = lambda i: i
    more = [] if out is None else [out]
    return call(
        functools.partial(close_kernel, scale),
        (count,),
        [planes(same), packed(same), packed(same)] + [ANY] * len(more),
        planes(lambda i: start + i),
        jax.ShapeDtypeStruct((2, ROWS, NG, NG), BF16),
        aliases={4: 0} if more else {},
    )(table, xo, so, zo, *more)


def placed(pieces):
    return [(sum(pieces[:k]), pieces[k]) for k in range(len(pieces))]


def shards(orbitals, plan):
    groups = lax.axis_size("band")
    core = lax.axis_index("band") % 2
    place = lax.axis_index("grid")
    moved = lambda step: [(g, step(g) % groups) for g in range(groups)]
    out_way = moved(lambda g: g - 2 if g % 2 == 0 else g + 2)
    home_way = moved(lambda g: g + 2 if g % 2 == 0 else g - 2)
    across = moved(lambda g: g + 1 if g % 2 == 0 else g - 1)
    exchange = lambda block: lax.all_to_all(block, "grid", split_axis=0, concat_axis=0, tiled=True)

    swapped = lax.ppermute(orbitals, "band", across)
    plan_left = lax.ppermute(lax.ppermute(plan, "band", across), "band", moved(lambda g: g + 3 if g % 2 == 0 else g - 3))
    table = jnp.concatenate(
        [jnp.where(core == 0, plan, plan_left).reshape(-1), core[None].astype(jnp.int32)]
    )
    arrived = []
    for start, count in placed(PIECES_IN):
        piece = pack(orbitals, start, count)
        arrived.append((start, count, lax.ppermute(piece, "band", out_way)))

    sines = sine_table()
    modes = jnp.arange(1, NG + 1, dtype=F32)
    root = decay(modes, modes)
    log_root = jnp.log2(root)
    local_modes = (place * ROWS + jnp.arange(1, ROWS + 1, dtype=jnp.int32)).astype(F32)
    root_local = decay(local_modes, modes)

    carried = None
    for start, count, z in arrived:
        carried = forward(table, orbitals, swapped, z, sines, root, log_root, carried, start, count)
    held, ends = carried
    edges = exchange(couple(table, root_local, exchange(ends)))

    scale = -((2.0 / (NG + 1)) ** 2)
    joined = jnp.concatenate([z for _, _, z in arrived], axis=1)
    u, parts = None, []
    for start, count in reversed(placed(PIECES_OUT)):
        if len(parts) in WAITS:
            xo, so, zo, *where = parts[-2]
            so, zo, u = lax.optimization_barrier((so, zo, u))
            parts[-2] = (xo, so, zo, *where)
        (xo, so, zo), u = back(table, orbitals, swapped, joined, sines, root, log_root, held, edges, u, start, count)
        parts.append((xo, lax.ppermute(so, "band", across), lax.ppermute(zo, "band", home_way), start, count))
    out = None
    for part in parts:
        xo, so, zo, start, count = part
        out = close(scale, table, xo, so, zo, out, start, count)
    return out


def solution(mesh):
    return jax.shard_map(
        shards,
        mesh=mesh,
        in_specs=(P("band", "grid", None, None), P(None, "band")),
        out_specs=P("band", "grid", None, None),
        check_vma=False,
    )
```

```python
import functools

import jax
import jax.numpy as jnp
from jax import lax
from jax.experimental import pallas as pl
from jax.experimental.pallas import tpu as pltpu
from jax.sharding import PartitionSpec as P

screening = 0.0005
NG = 192
SLABS = 8
ROWS = NG // SLABS
PAIRS = 4
WIDE = PAIRS * NG
PAIRED = ROWS // 2
PIECES_IN = (6, 4, 2)
PIECES_OUT = (1, 3, 3, 3, 2)
WAITS = (2,)

F32 = jnp.float32
BF16 = jnp.bfloat16
VMEM_LIMIT = 16 * 1024 * 1024

SWAP_BAND, THIRD_BAND, CORE = 0, 2, 4


def params():
    return pltpu.CompilerParams(vmem_limit_bytes=VMEM_LIMIT)


def call(kernel, grid, in_specs, out_specs, out_shape, scratch=(), aliases={}, cost=0):
    return pl.pallas_call(
        kernel,
        grid_spec=pltpu.PrefetchScalarGridSpec(
            num_scalar_prefetch=1, grid=grid, in_specs=in_specs, out_specs=out_specs, scratch_shapes=scratch
        ),
        out_shape=out_shape,
        input_output_aliases=aliases,
        compiler_params=params(),
        cost_estimate=pl.CostEstimate(flops=0, bytes_accessed=cost, transcendentals=0),
    )


def sine_table():
    counts = jnp.arange(1, NG + 1, dtype=F32)
    return jnp.sin(jnp.pi * counts[:, None] * counts[None, :] / (NG + 1)).astype(BF16)


def eigen_line(modes):
    half = jnp.sin(jnp.pi * modes / (2 * (NG + 1)))
    return 4.0 * half * half


def decay(first, second):
    mu = eigen_line(first)[:, None] + eigen_line(second)[None, :] + screening
    root = 1.0 / (1.0 + 0.5 * mu + jnp.sqrt(mu + 0.25 * mu * mu))
    return jnp.concatenate([root, root], axis=1)


def twice(block):
    return jnp.concatenate([block, block], axis=1)


def unpacked(ref, band, half):
    tail = ref[band, 0, 2].astype(F32)
    return jnp.concatenate([ref[band, 0, half].astype(F32), tail[:, 64 * half : 64 * half + 64]], axis=1)


def pack_into(ref, band, low, high):
    ref[band, 0, 0] = low[:, :128].astype(BF16)
    ref[band, 0, 1] = high[:, :128].astype(BF16)
    ref[band, 0, 2] = jnp.concatenate([low[:, 128:], high[:, 128:]], axis=1).astype(BF16)


def planes(block):
    return pl.BlockSpec((2, 2, NG, NG), lambda i, table: (0, block(i), 0, 0))


def packed(block):
    return pl.BlockSpec((2, 1, 3, NG, 128), lambda i, table: (0, block(i), 0, 0, 0))


def spectra(block):
    return pl.BlockSpec((2, NG, WIDE), lambda i, table: (block(i), 0, 0))


def whole(*shape):
    return pl.BlockSpec(shape, lambda i, table: (0,) * len(shape))


ANY = pl.BlockSpec(memory_space=pl.ANY)
STATE = jax.ShapeDtypeStruct((NG, WIDE), F32)


def in_hbm(block):
    return pltpu.with_memory_space_constraint(block, pltpu.HBM)


def pack_kernel(start, count, x_ref, z_ref, planes_in, packed_out, sems_in, sems_out):
    def fetch(i):
        return pltpu.make_async_copy(x_ref.at[:, pl.ds(2 * (start + i), 2)], planes_in.at[i], sems_in.at[i])

    def store(i):
        return pltpu.make_async_copy(packed_out.at[i], z_ref.at[:, i], sems_out.at[i])

    for i in range(count):
        fetch(i).start()
    for i in range(count):
        fetch(i).wait()
        for band in range(2):
            for half in range(2):
                packed_out[i, band, half] = planes_in[i, band, half, :, :128]
            tails = [planes_in[i, band, half, :, 128:].astype(F32) for half in range(2)]
            packed_out[i, band, 2] = jnp.concatenate(tails, axis=1).astype(BF16)
        store(i).start()
    for i in range(count):
        store(i).wait()


def pack(x, start, count):
    return pl.pallas_call(
        functools.partial(pack_kernel, start, count),
        in_specs=[ANY],
        out_specs=ANY,
        out_shape=jax.ShapeDtypeStruct((2, count, 3, NG, 128), BF16),
        scratch_shapes=[
            pltpu.VMEM((count, 2, 2, NG, NG), BF16),
            pltpu.VMEM((count, 2, 3, NG, 128), BF16),
            pltpu.SemaphoreType.DMA((count,)),
            pltpu.SemaphoreType.DMA((count,)),
        ],
        compiler_params=params(),
        cost_estimate=pl.CostEstimate(flops=0, bytes_accessed=0, transcendentals=0),
    )(in_hbm(x))


def forward_kernel(start, first, last, table, x_ref, s_ref, z_ref, sines_ref, r_ref, log_ref, *refs):
    refs = list(refs)
    if not first:
        p_in, a_in, _ = (refs.pop(0) for _ in range(3))
    out_ref = refs.pop(0)
    results = [refs.pop(0) for _ in range(1 if last else 2)]
    p_ref, a_ref, both = refs
    step = pl.program_id(0)

    @pl.when(step == 0)
    def _():
        p_ref[...] = jnp.zeros_like(p_ref) if first else p_in[...]
        a_ref[...] = jnp.zeros_like(a_ref) if first else a_in[...]

    core = table[CORE]
    sines = sines_ref[...]
    for half in range(2):
        for band in range(2):
            both[0, band] = x_ref[band, half]
            both[1, band] = unpacked(z_ref, band, half).astype(BF16)
        rows = [both[core, q] * s_ref[table[SWAP_BAND + q], half] for q in range(2)]
        rows += [both[core, q] * both[1 - core, table[THIRD_BAND + q]] for q in range(2)]
        section = jnp.dot(jnp.concatenate(rows, axis=0), sines, preferred_element_type=F32).astype(BF16)
        section = jnp.concatenate([section[q * NG : (q + 1) * NG] for q in range(PAIRS)], axis=1)
        section = jnp.dot(sines, section, preferred_element_type=F32)
        p = twice(r_ref[...]) * p_ref[...] + section
        p_ref[...] = p
        out_ref[half] = p.astype(BF16)
        depth = (2 * (start + step) + half).astype(F32)
        a_ref[...] += twice(jnp.exp2(depth * log_ref[...])) * section

    @pl.when(step == pl.num_programs(0) - 1)
    def _():
        if last:
            results[0][:, :WIDE] = a_ref[...].astype(BF16)
            results[0][:, WIDE:] = p_ref[...].astype(BF16)
        else:
            results[0][...] = p_ref[...]
            results[1][...] = a_ref[...]


def forward(table, x, s, z, sines, r, log_r, carried, start, count):
    first, last = carried is None, start + count == PAIRED
    at = lambda i: start + i
    return call(
        functools.partial(forward_kernel, start, first, last),
        (count,),
        [planes(at), planes(at), packed(lambda i: i), whole(NG, NG), whole(NG, 2 * NG), whole(NG, 2 * NG)]
        + ([] if first else [whole(NG, WIDE), whole(NG, WIDE), ANY]),
        [spectra(at)] + ([whole(NG, 2 * WIDE)] if last else [whole(NG, WIDE)] * 2),
        [pltpu.HBM((ROWS, NG, WIDE), BF16)] + ([pltpu.HBM((NG, 2 * WIDE), BF16)] if last else [STATE] * 2),
        scratch=[pltpu.VMEM((NG, WIDE), F32)] * 2 + [pltpu.VMEM((2, 2, NG, NG), BF16)],
        aliases={} if first else {9: 0},
    )(table, x, s, z, sines, r, log_r, *(() if first else (carried[1], carried[2], carried[0])))


def couple_kernel(table, r_ref, in_ref, out_ref):
    r = twice(r_ref[...])
    r2 = r * r
    r4 = r2 * r2
    r8 = r4 * r4
    span = r8 * r8 * r8
    gain = r / (1.0 - r2)
    part = lambda j, k: in_ref[j * ROWS : (j + 1) * ROWS, k * WIDE : (k + 1) * WIDE].astype(F32)
    reach = [jnp.ones_like(span)]
    left = [jnp.zeros_like(span)]
    for j in range(SLABS):
        reach.append(reach[-1] * span)
        left.append(span * left[-1] + part(j, 1))
    right = [jnp.zeros_like(span)]
    for j in reversed(range(SLABS)):
        right.insert(0, span * right[0] + part(j, 0))
    full = r * reach[SLABS]
    scale = r / (1.0 - full * full)
    low = scale * (full * left[SLABS] - right[0])
    high = gain * scale * (full * right[0] - left[SLABS])
    carry = [left[j] + low * reach[j] for j in range(SLABS)]
    for j in range(SLABS):
        out_ref[j * ROWS : (j + 1) * ROWS, :WIDE] = (r * carry[j]).astype(BF16)
        if j < SLABS - 1:
            beyond = gain * (r * carry[j + 1] + right[j + 1]) + high * reach[SLABS - 1 - j]
        else:
            beyond = jnp.zeros_like(span)
        out_ref[j * ROWS : (j + 1) * ROWS, WIDE:] = beyond.astype(BF16)


def couple(table, r_local, ends):
    return call(
        couple_kernel,
        (1,),
        [whole(ROWS, 2 * NG), whole(NG, 2 * WIDE)],
        whole(NG, 2 * WIDE),
        jax.ShapeDtypeStruct((NG, 2 * WIDE), BF16),
    )(table, r_local, ends)


def spread_terms(terms, places):
    apart = jnp.where(places[0] == places[1], 0.0, 1.0)
    other = apart * terms[1]
    return [terms[0] + (terms[1] - other), other]


def back_kernel(start, count, first, table, x_ref, s_ref, z_ref, sines_ref, r_ref, log_ref, p_ref, e_ref, *refs):
    refs = list(refs)
    if not first:
        u_in = refs.pop(0)
    xo_ref, so_ref, zo_ref = (refs.pop(0) for _ in range(3))
    if start > 0:
        u_out = refs.pop(0)
    u_ref, both = refs
    step = pl.program_id(0)

    @pl.when(step == 0)
    def _():
        u_ref[...] = e_ref[:, WIDE:].astype(F32) if first else u_in[...]

    core = table[CORE]
    low_core = core == 0
    sines = sines_ref[...]
    kept, given = {}, {}
    for half in (1, 0):
        for band in range(2):
            both[0, band] = x_ref[band, half]
            both[1, band] = unpacked(z_ref, band, half).astype(BF16)
        depth = (2 * (start + count - 1 - step) + half).astype(F32)
        carried = twice(jnp.exp2(depth * log_ref[...])) * e_ref[:, :WIDE].astype(F32)
        u = twice(r_ref[...]) * (p_ref[half].astype(F32) + u_ref[...] + carried)
        u_ref[...] = u
        section = jnp.dot(sines, u.astype(BF16), preferred_element_type=F32).astype(BF16)
        section = jnp.concatenate([section[:, q * NG : (q + 1) * NG] for q in range(PAIRS)], axis=0)
        potential = jnp.dot(section, sines, preferred_element_type=F32)
        v = [potential[q * NG : (q + 1) * NG] for q in range(PAIRS)]
        f = [both[core, q].astype(F32) for q in range(2)]
        s = [s_ref[table[SWAP_BAND + q], half].astype(F32) for q in range(2)]
        t = [both[1 - core, table[THIRD_BAND + q]].astype(F32) for q in range(2)]
        own = [v[q] * s[q] + v[2 + q] * t[q] for q in range(2)]
        swap = spread_terms([v[q] * f[q] for q in range(2)], [table[SWAP_BAND + q] for q in range(2)])
        third = spread_terms([v[2 + q] * f[q] for q in range(2)], [table[THIRD_BAND + q] for q in range(2)])
        swap_at, third_at = table[SWAP_BAND], table[THIRD_BAND]
        own_at, sent_at = jnp.where(low_core, 0, third_at), jnp.where(low_core, third_at, 0)
        for j in range(2):
            xo_ref[jnp.abs(own_at - j), half] = jnp.where(low_core, own[j], third[j]).astype(BF16)
            given[j, half] = swap[j]
            kept[j, half] = jnp.where(low_core, third[j], own[j])
    for j in range(2):
        pack_into(so_ref, jnp.abs(swap_at - j), given[j, 0], given[j, 1])
        pack_into(zo_ref, jnp.abs(sent_at - j), kept[j, 0], kept[j, 1])

    if start > 0:

        @pl.when(step == count - 1)
        def _():
            u_out[...] = u_ref[...]


def back(table, x, s, z, sines, r, log_r, p, edges, u, start, count):
    first = u is None
    at = lambda i: start + count - 1 - i
    local = lambda i: count - 1 - i
    outs = call(
        functools.partial(back_kernel, start, count, first),
        (count,),
        [
            planes(at),
            planes(at),
            packed(at),
            whole(NG, NG),
            whole(NG, 2 * NG),
            whole(NG, 2 * NG),
            spectra(at),
            whole(NG, 2 * WIDE),
        ]
        + ([] if first else [whole(NG, WIDE)]),
        [planes(local), packed(local), packed(local)] + ([whole(NG, WIDE)] if start > 0 else []),
        [jax.ShapeDtypeStruct((2, 2 * count, NG, NG), BF16)]
        + [jax.ShapeDtypeStruct((2, count, 3, NG, 128), BF16)] * 2
        + ([STATE] if start > 0 else []),
        scratch=[pltpu.VMEM((NG, WIDE), F32), pltpu.VMEM((2, 2, NG, NG), BF16)],
    )(table, *(in_hbm(block) for block in (x, s, z, sines, r, log_r, p, edges)), *(() if first else (u,)))
    return outs[:3], outs[3] if start > 0 else None


def close_kernel(scale, table, x_ref, s_ref, z_ref, *refs):
    for half in range(2):
        for band in range(2):
            total = x_ref[band, half].astype(F32) + unpacked(s_ref, band, half) + unpacked(z_ref, band, half)
            refs[-1][band, half] = (scale * total).astype(BF16)


def close(scale, table, xo, so, zo, out, start, count):
    same = lambda i: i
    more = [] if out is None else [out]
    return call(
        functools.partial(close_kernel, scale),
        (count,),
        [planes(same), packed(same), packed(same)] + [ANY] * len(more),
        planes(lambda i: start + i),
        jax.ShapeDtypeStruct((2, ROWS, NG, NG), BF16),
        aliases={4: 0} if more else {},
    )(table, xo, so, zo, *more)


def placed(pieces):
    return [(sum(pieces[:k]), pieces[k]) for k in range(len(pieces))]


def shards(orbitals, plan):
    groups = lax.axis_size("band")
    core = lax.axis_index("band") % 2
    place = lax.axis_index("grid")
    moved = lambda step: [(g, step(g) % groups) for g in range(groups)]
    out_way = moved(lambda g: g - 2 if g % 2 == 0 else g + 2)
    home_way = moved(lambda g: g + 2 if g % 2 == 0 else g - 2)
    across = moved(lambda g: g + 1 if g % 2 == 0 else g - 1)
    exchange = lambda block: lax.all_to_all(block, "grid", split_axis=0, concat_axis=0, tiled=True)

    swapped = lax.ppermute(orbitals, "band", across)
    plan_left = lax.ppermute(lax.ppermute(plan, "band", across), "band", moved(lambda g: g + 3 if g % 2 == 0 else g - 3))
    table = jnp.concatenate(
        [jnp.where(core == 0, plan, plan_left).reshape(-1), core[None].astype(jnp.int32)]
    )
    arrived = []
    for start, count in placed(PIECES_IN):
        piece = pack(orbitals, start, count)
        arrived.append((start, count, lax.ppermute(piece, "band", out_way)))

    sines = sine_table()
    modes = jnp.arange(1, NG + 1, dtype=F32)
    root = decay(modes, modes)
    log_root = jnp.log2(root)
    local_modes = (place * ROWS + jnp.arange(1, ROWS + 1, dtype=jnp.int32)).astype(F32)
    root_local = decay(local_modes, modes)

    carried = None
    for start, count, z in arrived:
        carried = forward(table, orbitals, swapped, z, sines, root, log_root, carried, start, count)
    held, ends = carried
    edges = exchange(couple(table, root_local, exchange(ends)))

    scale = -((2.0 / (NG + 1)) ** 2)
    joined = jnp.concatenate([z for _, _, z in arrived], axis=1)
    u, parts = None, []
    for start, count in reversed(placed(PIECES_OUT)):
        if len(parts) in WAITS:
            xo, so, zo, *where = parts[-2]
            so, zo, u = lax.optimization_barrier((so, zo, u))
            parts[-2] = (xo, so, zo, *where)
        (xo, so, zo), u = back(table, orbitals, swapped, joined, sines, root, log_root, held, edges, u, start, count)
        parts.append((xo, lax.ppermute(so, "band", across), lax.ppermute(zo, "band", home_way), start, count))
    out = None
    for part in parts:
        xo, so, zo, start, count = part
        out = close(scale, table, xo, so, zo, out, start, count)
    return out


def solution(mesh):
    return jax.shard_map(
        shards,
        mesh=mesh,
        in_specs=(P("band", "grid", None, None), P(None, "band")),
        out_specs=P("band", "grid", None, None),
        check_vma=False,
    )
```

```python
import functools

import jax
import jax.numpy as jnp
from jax import lax
from jax.experimental import pallas as pl
from jax.experimental.pallas import tpu as pltpu
from jax.sharding import PartitionSpec as P

screening = 0.0005
NG = 192
SLABS = 8
ROWS = NG // SLABS
PAIRS = 4
WIDE = PAIRS * NG
PAIRED = ROWS // 2
PIECES_IN = (6, 4, 2)
PIECES_OUT = (1, 1, 4, 4, 2)
WAITS = (2,)

F32 = jnp.float32
BF16 = jnp.bfloat16
VMEM_LIMIT = 16 * 1024 * 1024

SWAP_BAND, THIRD_BAND, CORE = 0, 2, 4


def params():
    return pltpu.CompilerParams(vmem_limit_bytes=VMEM_LIMIT)


def call(kernel, grid, in_specs, out_specs, out_shape, scratch=(), aliases={}, cost=0):
    return pl.pallas_call(
        kernel,
        grid_spec=pltpu.PrefetchScalarGridSpec(
            num_scalar_prefetch=1, grid=grid, in_specs=in_specs, out_specs=out_specs, scratch_shapes=scratch
        ),
        out_shape=out_shape,
        input_output_aliases=aliases,
        compiler_params=params(),
        cost_estimate=pl.CostEstimate(flops=0, bytes_accessed=cost, transcendentals=0),
    )


def sine_table():
    counts = jnp.arange(1, NG + 1, dtype=F32)
    return jnp.sin(jnp.pi * counts[:, None] * counts[None, :] / (NG + 1)).astype(BF16)


def eigen_line(modes):
    half = jnp.sin(jnp.pi * modes / (2 * (NG + 1)))
    return 4.0 * half * half


def decay(first, second):
    mu = eigen_line(first)[:, None] + eigen_line(second)[None, :] + screening
    root = 1.0 / (1.0 + 0.5 * mu + jnp.sqrt(mu + 0.25 * mu * mu))
    return jnp.concatenate([root, root], axis=1)


def twice(block):
    return jnp.concatenate([block, block], axis=1)


def unpacked(ref, band, half):
    tail = ref[band, 0, 2].astype(F32)
    return jnp.concatenate([ref[band, 0, half].astype(F32), tail[:, 64 * half : 64 * half + 64]], axis=1)


def pack_into(ref, band, low, high):
    ref[band, 0, 0] = low[:, :128].astype(BF16)
    ref[band, 0, 1] = high[:, :128].astype(BF16)
    ref[band, 0, 2] = jnp.concatenate([low[:, 128:], high[:, 128:]], axis=1).astype(BF16)


def planes(block):
    return pl.BlockSpec((2, 2, NG, NG), lambda i, table: (0, block(i), 0, 0))


def packed(block):
    return pl.BlockSpec((2, 1, 3, NG, 128), lambda i, table: (0, block(i), 0, 0, 0))


def spectra(block):
    return pl.BlockSpec((2, NG, WIDE), lambda i, table: (block(i), 0, 0))


def whole(*shape):
    return pl.BlockSpec(shape, lambda i, table: (0,) * len(shape))


ANY = pl.BlockSpec(memory_space=pl.ANY)
STATE = jax.ShapeDtypeStruct((NG, WIDE), F32)


def in_hbm(block):
    return pltpu.with_memory_space_constraint(block, pltpu.HBM)


def pack_kernel(start, count, x_ref, z_ref, planes_in, packed_out, sems_in, sems_out):
    def fetch(i):
        return pltpu.make_async_copy(x_ref.at[:, pl.ds(2 * (start + i), 2)], planes_in.at[i], sems_in.at[i])

    def store(i):
        return pltpu.make_async_copy(packed_out.at[i], z_ref.at[:, i], sems_out.at[i])

    for i in range(count):
        fetch(i).start()
    for i in range(count):
        fetch(i).wait()
        for band in range(2):
            for half in range(2):
                packed_out[i, band, half] = planes_in[i, band, half, :, :128]
            tails = [planes_in[i, band, half, :, 128:].astype(F32) for half in range(2)]
            packed_out[i, band, 2] = jnp.concatenate(tails, axis=1).astype(BF16)
        store(i).start()
    for i in range(count):
        store(i).wait()


def pack(x, start, count):
    return pl.pallas_call(
        functools.partial(pack_kernel, start, count),
        in_specs=[ANY],
        out_specs=ANY,
        out_shape=jax.ShapeDtypeStruct((2, count, 3, NG, 128), BF16),
        scratch_shapes=[
            pltpu.VMEM((count, 2, 2, NG, NG), BF16),
            pltpu.VMEM((count, 2, 3, NG, 128), BF16),
            pltpu.SemaphoreType.DMA((count,)),
            pltpu.SemaphoreType.DMA((count,)),
        ],
        compiler_params=params(),
        cost_estimate=pl.CostEstimate(flops=0, bytes_accessed=0, transcendentals=0),
    )(in_hbm(x))


def forward_kernel(start, first, last, table, x_ref, s_ref, z_ref, sines_ref, r_ref, log_ref, *refs):
    refs = list(refs)
    if not first:
        p_in, a_in, _ = (refs.pop(0) for _ in range(3))
    out_ref = refs.pop(0)
    results = [refs.pop(0) for _ in range(1 if last else 2)]
    p_ref, a_ref, both = refs
    step = pl.program_id(0)

    @pl.when(step == 0)
    def _():
        p_ref[...] = jnp.zeros_like(p_ref) if first else p_in[...]
        a_ref[...] = jnp.zeros_like(a_ref) if first else a_in[...]

    core = table[CORE]
    sines = sines_ref[...]
    for half in range(2):
        for band in range(2):
            both[0, band] = x_ref[band, half]
            both[1, band] = unpacked(z_ref, band, half).astype(BF16)
        rows = [both[core, q] * s_ref[table[SWAP_BAND + q], half] for q in range(2)]
        rows += [both[core, q] * both[1 - core, table[THIRD_BAND + q]] for q in range(2)]
        section = jnp.dot(jnp.concatenate(rows, axis=0), sines, preferred_element_type=F32).astype(BF16)
        section = jnp.concatenate([section[q * NG : (q + 1) * NG] for q in range(PAIRS)], axis=1)
        section = jnp.dot(sines, section, preferred_element_type=F32)
        p = twice(r_ref[...]) * p_ref[...] + section
        p_ref[...] = p
        out_ref[half] = p.astype(BF16)
        depth = (2 * (start + step) + half).astype(F32)
        a_ref[...] += twice(jnp.exp2(depth * log_ref[...])) * section

    @pl.when(step == pl.num_programs(0) - 1)
    def _():
        if last:
            results[0][:, :WIDE] = a_ref[...].astype(BF16)
            results[0][:, WIDE:] = p_ref[...].astype(BF16)
        else:
            results[0][...] = p_ref[...]
            results[1][...] = a_ref[...]


def forward(table, x, s, z, sines, r, log_r, carried, start, count):
    first, last = carried is None, start + count == PAIRED
    at = lambda i: start + i
    return call(
        functools.partial(forward_kernel, start, first, last),
        (count,),
        [planes(at), planes(at), packed(lambda i: i), whole(NG, NG), whole(NG, 2 * NG), whole(NG, 2 * NG)]
        + ([] if first else [whole(NG, WIDE), whole(NG, WIDE), ANY]),
        [spectra(at)] + ([whole(NG, 2 * WIDE)] if last else [whole(NG, WIDE)] * 2),
        [pltpu.HBM((ROWS, NG, WIDE), BF16)] + ([pltpu.HBM((NG, 2 * WIDE), BF16)] if last else [STATE] * 2),
        scratch=[pltpu.VMEM((NG, WIDE), F32)] * 2 + [pltpu.VMEM((2, 2, NG, NG), BF16)],
        aliases={} if first else {9: 0},
    )(table, x, s, z, sines, r, log_r, *(() if first else (carried[1], carried[2], carried[0])))


def couple_kernel(table, r_ref, in_ref, out_ref):
    r = twice(r_ref[...])
    r2 = r * r
    r4 = r2 * r2
    r8 = r4 * r4
    span = r8 * r8 * r8
    gain = r / (1.0 - r2)
    part = lambda j, k: in_ref[j * ROWS : (j + 1) * ROWS, k * WIDE : (k + 1) * WIDE].astype(F32)
    reach = [jnp.ones_like(span)]
    left = [jnp.zeros_like(span)]
    for j in range(SLABS):
        reach.append(reach[-1] * span)
        left.append(span * left[-1] + part(j, 1))
    right = [jnp.zeros_like(span)]
    for j in reversed(range(SLABS)):
        right.insert(0, span * right[0] + part(j, 0))
    full = r * reach[SLABS]
    scale = r / (1.0 - full * full)
    low = scale * (full * left[SLABS] - right[0])
    high = gain * scale * (full * right[0] - left[SLABS])
    carry = [left[j] + low * reach[j] for j in range(SLABS)]
    for j in range(SLABS):
        out_ref[j * ROWS : (j + 1) * ROWS, :WIDE] = (r * carry[j]).astype(BF16)
        if j < SLABS - 1:
            beyond = gain * (r * carry[j + 1] + right[j + 1]) + high * reach[SLABS - 1 - j]
        else:
            beyond = jnp.zeros_like(span)
        out_ref[j * ROWS : (j + 1) * ROWS, WIDE:] = beyond.astype(BF16)


def couple(table, r_local, ends):
    return call(
        couple_kernel,
        (1,),
        [whole(ROWS, 2 * NG), whole(NG, 2 * WIDE)],
        whole(NG, 2 * WIDE),
        jax.ShapeDtypeStruct((NG, 2 * WIDE), BF16),
    )(table, r_local, ends)


def spread_terms(terms, places):
    apart = jnp.where(places[0] == places[1], 0.0, 1.0)
    other = apart * terms[1]
    return [terms[0] + (terms[1] - other), other]


def back_kernel(start, count, first, table, x_ref, s_ref, z_ref, sines_ref, r_ref, log_ref, p_ref, e_ref, *refs):
    refs = list(refs)
    if not first:
        u_in = refs.pop(0)
    xo_ref, so_ref, zo_ref = (refs.pop(0) for _ in range(3))
    if start > 0:
        u_out = refs.pop(0)
    u_ref, both = refs
    step = pl.program_id(0)

    @pl.when(step == 0)
    def _():
        u_ref[...] = e_ref[:, WIDE:].astype(F32) if first else u_in[...]

    core = table[CORE]
    low_core = core == 0
    sines = sines_ref[...]
    kept, given = {}, {}
    for half in (1, 0):
        for band in range(2):
            both[0, band] = x_ref[band, half]
            both[1, band] = unpacked(z_ref, band, half).astype(BF16)
        depth = (2 * (start + count - 1 - step) + half).astype(F32)
        carried = twice(jnp.exp2(depth * log_ref[...])) * e_ref[:, :WIDE].astype(F32)
        u = twice(r_ref[...]) * (p_ref[half].astype(F32) + u_ref[...] + carried)
        u_ref[...] = u
        section = jnp.dot(sines, u.astype(BF16), preferred_element_type=F32).astype(BF16)
        section = jnp.concatenate([section[:, q * NG : (q + 1) * NG] for q in range(PAIRS)], axis=0)
        potential = jnp.dot(section, sines, preferred_element_type=F32)
        v = [potential[q * NG : (q + 1) * NG] for q in range(PAIRS)]
        f = [both[core, q].astype(F32) for q in range(2)]
        s = [s_ref[table[SWAP_BAND + q], half].astype(F32) for q in range(2)]
        t = [both[1 - core, table[THIRD_BAND + q]].astype(F32) for q in range(2)]
        own = [v[q] * s[q] + v[2 + q] * t[q] for q in range(2)]
        swap = spread_terms([v[q] * f[q] for q in range(2)], [table[SWAP_BAND + q] for q in range(2)])
        third = spread_terms([v[2 + q] * f[q] for q in range(2)], [table[THIRD_BAND + q] for q in range(2)])
        swap_at, third_at = table[SWAP_BAND], table[THIRD_BAND]
        own_at, sent_at = jnp.where(low_core, 0, third_at), jnp.where(low_core, third_at, 0)
        for j in range(2):
            xo_ref[jnp.abs(own_at - j), half] = jnp.where(low_core, own[j], third[j]).astype(BF16)
            given[j, half] = swap[j]
            kept[j, half] = jnp.where(low_core, third[j], own[j])
    for j in range(2):
        pack_into(so_ref, jnp.abs(swap_at - j), given[j, 0], given[j, 1])
        pack_into(zo_ref, jnp.abs(sent_at - j), kept[j, 0], kept[j, 1])

    if start > 0:

        @pl.when(step == count - 1)
        def _():
            u_out[...] = u_ref[...]


def back(table, x, s, z, sines, r, log_r, p, edges, u, start, count):
    first = u is None
    at = lambda i: start + count - 1 - i
    local = lambda i: count - 1 - i
    outs = call(
        functools.partial(back_kernel, start, count, first),
        (count,),
        [
            planes(at),
            planes(at),
            packed(at),
            whole(NG, NG),
            whole(NG, 2 * NG),
            whole(NG, 2 * NG),
            spectra(at),
            whole(NG, 2 * WIDE),
        ]
        + ([] if first else [whole(NG, WIDE)]),
        [planes(local), packed(local), packed(local)] + ([whole(NG, WIDE)] if start > 0 else []),
        [jax.ShapeDtypeStruct((2, 2 * count, NG, NG), BF16)]
        + [jax.ShapeDtypeStruct((2, count, 3, NG, 128), BF16)] * 2
        + ([STATE] if start > 0 else []),
        scratch=[pltpu.VMEM((NG, WIDE), F32), pltpu.VMEM((2, 2, NG, NG), BF16)],
    )(table, *(in_hbm(block) for block in (x, s, z, sines, r, log_r, p, edges)), *(() if first else (u,)))
    return outs[:3], outs[3] if start > 0 else None


def close_kernel(scale, table, x_ref, s_ref, z_ref, *refs):
    for half in range(2):
        for band in range(2):
            total = x_ref[band, half].astype(F32) + unpacked(s_ref, band, half) + unpacked(z_ref, band, half)
            refs[-1][band, half] = (scale * total).astype(BF16)


def close(scale, table, xo, so, zo, out, start, count):
    same = lambda i: i
    more = [] if out is None else [out]
    return call(
        functools.partial(close_kernel, scale),
        (count,),
        [planes(same), packed(same), packed(same)] + [ANY] * len(more),
        planes(lambda i: start + i),
        jax.ShapeDtypeStruct((2, ROWS, NG, NG), BF16),
        aliases={4: 0} if more else {},
    )(table, xo, so, zo, *more)


def placed(pieces):
    return [(sum(pieces[:k]), pieces[k]) for k in range(len(pieces))]


def shards(orbitals, plan):
    groups = lax.axis_size("band")
    core = lax.axis_index("band") % 2
    place = lax.axis_index("grid")
    moved = lambda step: [(g, step(g) % groups) for g in range(groups)]
    out_way = moved(lambda g: g - 2 if g % 2 == 0 else g + 2)
    home_way = moved(lambda g: g + 2 if g % 2 == 0 else g - 2)
    across = moved(lambda g: g + 1 if g % 2 == 0 else g - 1)
    exchange = lambda block: lax.all_to_all(block, "grid", split_axis=0, concat_axis=0, tiled=True)

    swapped = lax.ppermute(orbitals, "band", across)
    plan_left = lax.ppermute(lax.ppermute(plan, "band", across), "band", moved(lambda g: g + 3 if g % 2 == 0 else g - 3))
    table = jnp.concatenate(
        [jnp.where(core == 0, plan, plan_left).reshape(-1), core[None].astype(jnp.int32)]
    )
    arrived = []
    for start, count in placed(PIECES_IN):
        piece = pack(orbitals, start, count)
        arrived.append((start, count, lax.ppermute(piece, "band", out_way)))

    sines = sine_table()
    modes = jnp.arange(1, NG + 1, dtype=F32)
    root = decay(modes, modes)
    log_root = jnp.log2(root)
    local_modes = (place * ROWS + jnp.arange(1, ROWS + 1, dtype=jnp.int32)).astype(F32)
    root_local = decay(local_modes, modes)

    carried = None
    for start, count, z in arrived:
        carried = forward(table, orbitals, swapped, z, sines, root, log_root, carried, start, count)
    held, ends = carried
    edges = exchange(couple(table, root_local, exchange(ends)))

    scale = -((2.0 / (NG + 1)) ** 2)
    joined = jnp.concatenate([z for _, _, z in arrived], axis=1)
    u, parts = None, []
    for start, count in reversed(placed(PIECES_OUT)):
        if len(parts) in WAITS:
            xo, so, zo, *where = parts[-2]
            so, zo, u = lax.optimization_barrier((so, zo, u))
            parts[-2] = (xo, so, zo, *where)
        (xo, so, zo), u = back(table, orbitals, swapped, joined, sines, root, log_root, held, edges, u, start, count)
        parts.append((xo, lax.ppermute(so, "band", across), lax.ppermute(zo, "band", home_way), start, count))
    out = None
    for part in parts:
        xo, so, zo, start, count = part
        out = close(scale, table, xo, so, zo, out, start, count)
    return out


def solution(mesh):
    return jax.shard_map(
        shards,
        mesh=mesh,
        in_specs=(P("band", "grid", None, None), P(None, "band")),
        out_specs=P("band", "grid", None, None),
        check_vma=False,
    )
```
